32 devices in a mesh: dom: 2 (over x), tok: 16 (over z, y, core).
Axes of the slice: x: 2, y: 2, z: 4, core: 2. Of those that a mesh axis runs over, the one named last changes fastest.
Arguments:
- tokens: bfloat16 [512, 4096], P(('dom', 'tok')), parts along dimension 0, may hold values from -6 to 6
- rotation_flip: int32 [4096], replicated, may hold values from 0 to 1
- gate_up: bfloat16 [4, 4096, 16384], P('dom', None, 'tok'), parts along dimension 0, may hold values from -0.09375 to 0.09375
- quant_codes: bfloat16 [4, 4096, 16384], P('dom', None, 'tok'), parts along dimension 0, may hold values from -7 to 7
- quant_exps: int32 [4, 32, 16384], P('dom', None, 'tok'), parts along dimension 0, may hold values from -10 to -7
- down_rows: bfloat16 [32768, 4096], P(('dom', 'tok')), parts along dimension 0, may hold values from -0.046875 to 0.046875
Outputs:
- correction: bfloat16 [32768, 4096], P(('dom', 'tok')), parts along dimension 0
The draws below stay inside these ranges and needn't reach their ends.
There are 2 independent parts, one for each index of `dom`. The reference program is written for one: setup_inputs(seed, part) draws one part's arguments, and reference() takes and returns one part's arrays. A program takes and returns all parts, laid end to end along the dimension named above; an argument that names none is the same for every part. Nothing has to cross between parts.
All inputs are finite; a program needn't handle non-finite values.
Results may differ from the reference program's by a relative error of at most 0.012.
Values may be sent and summed in bfloat16 or wider, within the bound.
A program may use at most 128 MiB of HBM per device.

```python
import jax
import jax.numpy as jnp
from jax import lax

D = 4096
FF = 16384
DO = 4096
GROUP = 128
TOKENS = 256


def draw_quant_codes(key, part):
    return jax.random.randint(key, (2, D, FF), -7, 8).astype(jnp.float32).astype(jnp.bfloat16)


def set_ends(values, key, low, largest):
    spot = [jax.random.randint(jax.random.fold_in(key, axis), (), 0, length) for axis, length in enumerate(values.shape)]
    widest = values.shape.index(max(values.shape))
    neighbour = spot[:widest] + [(spot[widest] + 1) % values.shape[widest]] + spot[widest + 1:]
    return values.at[tuple(spot)].set(low).at[tuple(neighbour)].set(largest)


def block_scale(own_key, dims, cuts, least, largest):
    def one(dim, blocks):
        steps = jax.random.uniform(jax.random.fold_in(jax.random.fold_in(own_key, 6), dim), (blocks,), jnp.float32, least / len(cuts), largest / len(cuts))
        return jnp.repeat(jnp.exp(steps), dims[dim] // blocks).reshape((-1,) + (1,) * (len(dims) - dim - 1))

    factor_of = one(*cuts[0])
    for cut in cuts[1:]:
        factor_of = factor_of * one(*cut)
    return factor_of


def gaussian(own_key, dims, scale, limit, shards=(), held_as=jnp.bfloat16):
    array = scale * jax.random.normal(own_key, dims, jnp.float32)
    if shards:
        array = array * block_scale(own_key, dims, shards, -0.22, 0.18)
    return jnp.clip(array, -limit, limit).astype(held_as)


def setup_inputs(seed: int = 0, part: int = 0) -> dict:
    splits = jax.random.split(jax.random.key(seed), 7)
    part_keys = jax.random.split(jax.random.fold_in(splits[6], part), 7)
    return {
        "tokens": gaussian(part_keys[0], (TOKENS, D), 1.0, 6.0, ((0, 16),)),
        "rotation_flip": set_ends(jax.random.randint(splits[1], (D,), 0, 2), jax.random.fold_in(splits[1], 1), 0, 1).astype(jnp.int32),
        "gate_up": gaussian(part_keys[2], (2, D, FF), D ** -0.5, 0.09375, ((2, 16),)),
        "quant_codes": draw_quant_codes(jax.random.fold_in(jax.random.fold_in(splits[6], part), 71), part),
        "quant_exps": set_ends(jax.random.randint(part_keys[4], (2, D // GROUP, FF), -10, -6), jax.random.fold_in(part_keys[4], 1), -10, (-6) - 1).astype(jnp.int32),
        "down_rows": gaussian(part_keys[5], (FF, DO), FF ** -0.5, 0.046875, ((0, 16),)),
    }


def hadamard_table(order):
    index = jnp.arange(order, dtype=jnp.int32)
    common = index[:, None] & index[None, :]
    parity = jnp.zeros((order, order), jnp.int32)
    for bit_pos in range(max(order.bit_length() - 1, 1)):
        parity = parity ^ ((common >> bit_pos) & 1)
    return (1 - 2 * parity).astype(jnp.float32)


def rotate(inputs, flip):
    width = inputs.shape[-1]
    signed = inputs.astype(jnp.float32) * (1 - 2 * flip).astype(jnp.float32)
    power = width.bit_length() - 1
    outer_len = 2 ** (power // 2)
    inner_len = width // outer_len
    blocks = signed.reshape(-1, outer_len, inner_len)
    mixed = jnp.einsum("ab,nbc,cd->nad", hadamard_table(outer_len), blocks, hadamard_table(inner_len), precision=lax.Precision.HIGHEST)
    return (mixed.reshape(-1, width) * (1.0 / (width ** 0.5))).astype(jnp.bfloat16)


def dequant(codes, exps):
    groups = exps.shape[1]
    scales = jnp.exp2(exps.astype(jnp.float32))
    shaped = codes.astype(jnp.float32).reshape(2, groups, codes.shape[1] // groups, codes.shape[2])
    return (shaped * scales[:, :, None, :]).reshape(codes.shape).astype(jnp.bfloat16)


def swiglu(inputs, weights):
    gate = jnp.dot(inputs, weights[0], preferred_element_type=jnp.float32)
    upper = jnp.dot(inputs, weights[1], preferred_element_type=jnp.float32)
    return (jax.nn.silu(gate) * upper).astype(jnp.bfloat16)


def reference(tokens, rotation_flip, gate_up, quant_codes, quant_exps, down_rows):
    rotated = rotate(tokens, rotation_flip)
    quant_weight = dequant(quant_codes, quant_exps)
    hid_full = swiglu(tokens, gate_up)
    hid_quant = swiglu(rotated, quant_weight)
    mismatch = (hid_full.astype(jnp.float32) - hid_quant.astype(jnp.float32)).astype(jnp.bfloat16)
    projected = jnp.dot(mismatch, down_rows, preferred_element_type=jnp.float32).astype(jnp.bfloat16)
    gram = lax.dot_general(hid_quant, projected, (((0,), (0,)), ((), ())), preferred_element_type=jnp.float32)
    return (gram * (1.0 / (tokens.shape[0] ** 0.5))).astype(jnp.bfloat16)
```

```python
import functools

import jax
import jax.numpy as jnp
import numpy as np
from jax import lax
from jax.experimental import pallas as pl
from jax.experimental.pallas import tpu as pltpu
from jax.sharding import PartitionSpec as P

MESH = pl.DeviceIdType.MESH
F32 = jnp.float32
BF16 = jnp.bfloat16


def hadamard_block(order):
    index = np.arange(order)
    common = index[:, None] & index[None, :]
    parity = np.zeros((order, order), np.int32)
    for bit_pos in range(order.bit_length()):
        parity ^= (common >> bit_pos) & 1
    return (1 - 2 * parity).astype(np.float32)


def xor(value, mask):
    out, bit = value, 1
    while bit <= mask:
        if mask & bit:
            out = out + bit * (1 - 2 * ((value // bit) % 2))
        bit *= 2
    return out


def kernel(
    n, group,
    tok_ref, flip_ref, had_ref, exps_ref, gu_hbm, codes_hbm, down_hbm,
    hidq_ref, proj_hbm,
    gu_v, codes_v, down_v, tok_v, rot_v, mis_v, proj_v,
    csend, crecv, ysend, yrecv, zsend, zrecv,
    codes_sem, gu_sem, down_sem, out_sem,
    az_s, az_r, ay_s, ay_r, ac_s, ac_r,
    bz_s, bz_r, by_s, by_r, bc_s, bc_r,
    rz_s, rz_r, ry_s, ry_r, rc_s, rc_r,
):
    nz = n // 4
    me = lax.axis_index("tok")
    z, y, c = me // 4, (me // 2) % 2, me % 2
    own_rows, width = tok_ref.shape
    tokens = own_rows * n
    hidden = mis_v.shape[1]
    cols = proj_v.shape[1] // n

    def index(zz, yy, cc):
        return (zz * 2 + yy) * 2 + cc

    zs = [xor(z, k) for k in range(nz)]
    z_peer = [index(zs[k], y, c) for k in range(nz)]
    y_peer, c_peer = index(z, 1 - y, c), index(z, y, 1 - c)

    chunks = codes_sem.shape[1]
    depth = width // chunks
    code_copies = [
        pltpu.make_async_copy(
            codes_hbm.at[p, pl.ds(q * depth, depth)],
            codes_v.at[p, pl.ds(q * depth, depth)],
            codes_sem.at[p, q],
        )
        for p in range(2) for q in range(chunks)
    ]
    gu_copies = [
        pltpu.make_async_copy(gu_hbm.at[p], gu_v.at[p], gu_sem.at[p]) for p in range(2)
    ]
    down_copy = pltpu.make_async_copy(down_hbm, down_v, down_sem)
    for copy in code_copies + gu_copies + [down_copy]:
        copy.start()

    def row_block(i):
        return tok_v.at[pl.ds(pl.multiple_of(i * own_rows, own_rows), own_rows)]

    def col_block(i):
        return proj_v.at[:, pl.ds(pl.multiple_of(i * cols, cols), cols)]

    row_block(me)[...] = tok_ref[...]

    barrier = pltpu.get_barrier_semaphore()
    peers = z_peer[1:] + [y_peer, c_peer]
    for peer in peers:
        pl.semaphore_signal(barrier, inc=1, device_id={"tok": peer}, device_id_type=MESH)
    pl.semaphore_wait(barrier, len(peers))

    sent = []

    def send(src, dst, ssem, rsem, peer):
        copy = pltpu.make_async_remote_copy(
            src_ref=src, dst_ref=dst, send_sem=ssem, recv_sem=rsem,
            device_id={"tok": peer}, device_id_type=MESH,
        )
        copy.start()
        sent.append(copy)

    def arrived(dst, ssem, rsem, peer):
        pltpu.make_async_remote_copy(
            src_ref=dst, dst_ref=dst, send_sem=ssem, recv_sem=rsem,
            device_id={"tok": peer}, device_id_type=MESH,
        ).wait_recv()

    def gather(block, sems, between, landed):
        z_s, z_r, y_s, y_r, c_s, c_r = sems

        def on_y(k):
            i = index(zs[k], 1 - y, c)
            arrived(block(i), y_s.at[k], y_r.at[k], y_peer)
            send(block(i), block(i), c_s.at[k, 1], c_r.at[k, 1], c_peer)
            landed(i)

        def out(k):
            i = z_peer[k]
            send(block(i), block(i), y_s.at[k], y_r.at[k], y_peer)
            send(block(i), block(i), c_s.at[k, 0], c_r.at[k, 0], c_peer)
            landed(i)

        for k in range(nz - 1, 0, -1):
            send(block(me), block(me), z_s.at[k], z_r.at[k], z_peer[k])
        out(0)
        between(0)
        for k in range(1, nz):
            arrived(block(z_peer[k]), z_s.at[k], z_r.at[k], z_peer[k])
            out(k)
            on_y(k - 1)
            between(k)
        on_y(nz - 1)
        for k in range(nz):
            for s in range(2):
                i = index(zs[k], y + s * (1 - 2 * y), 1 - c)
                arrived(block(i), c_s.at[k, s], c_r.at[k, s], c_peer)
                landed(i)

    def scale_chunk(t):
        p, q = t // chunks, t % chunks
        code_copies[t].wait()

        def one(step, carry):
            g = q * (depth // group) + step
            scale = jnp.exp2(exps_ref[p, pl.ds(g, 1), :].astype(F32))
            tile = jnp.broadcast_to(scale, (16, hidden)).astype(BF16)
            for r in range(group // 16):
                rows = pl.ds(pl.multiple_of(g * group + r * 16, 16), 16)
                codes_v[p, rows, :] = codes_v[p, rows, :] * tile
            return carry

        lax.fori_loop(0, depth // group, one, 0)

    total = 2 * chunks
    marks = [total // 2 + (total - total // 2) * k // (nz - 1) for k in range(nz)]

    def between(k):
        for t in range(marks[k - 1] if k else 0, marks[k]):
            scale_chunk(t)

    gather(row_block, (az_s, az_r, ay_s, ay_r, ac_s, ac_r), between, lambda i: None)

    had = had_ref.shape[0]
    sign = (1 - 2 * flip_ref[...]).astype(F32).astype(BF16)
    table = had_ref[...]
    span = min(64, tokens)

    def rotate(step, carry):
        rows = pl.ds(pl.multiple_of(step * span, span), span)
        parts = []
        for b in range(width // had):
            lanes = slice(b * had, (b + 1) * had)
            signed = tok_v[rows, lanes] * sign[:, lanes]
            parts.append(jnp.dot(signed, table, preferred_element_type=F32))
        half = 1
        while half < len(parts):
            for b in range(len(parts)):
                if not b & half:
                    low, high = parts[b], parts[b + half]
                    parts[b], parts[b + half] = low + high, low - high
            half *= 2
        for b in range(width // had):
            rot_v[rows, b * had:(b + 1) * had] = (parts[b] * (1.0 / width**0.5)).astype(BF16)
        return carry

    lax.fori_loop(0, tokens // span, rotate, 0)

    for copy in gu_copies:
        copy.wait()
    tile = 256

    def swiglu(lhs, w, lanes):
        gate = jnp.dot(lhs[...], w[0, :, lanes], preferred_element_type=F32)
        upper = jnp.dot(lhs[...], w[1, :, lanes], preferred_element_type=F32)
        return (gate / (1.0 + jnp.exp(-gate)) * upper).astype(BF16)

    def hidden_tile(step, carry):
        lanes = pl.ds(pl.multiple_of(step * tile, tile), tile)
        full = swiglu(tok_v, gu_v, lanes)
        quant = swiglu(rot_v, codes_v, lanes)
        hidq_ref[:, lanes] = quant
        mis_v[:, lanes] = (full.astype(F32) - quant.astype(F32)).astype(BF16)
        return carry

    lax.fori_loop(0, hidden // tile, hidden_tile, 0)

    down_copy.wait()

    def partial(i):
        lanes = pl.ds(pl.multiple_of(i * cols, cols), cols)
        return jnp.dot(mis_v[...], down_v[:, lanes], preferred_element_type=F32)

    order = list(range(nz - 1, -1, -1))

    def to_core(k, s):
        yy = y + s * (1 - 2 * y)
        csend[k, s] = partial(index(zs[k], yy, 1 - c)).astype(BF16)
        send(csend.at[k, s], crecv.at[k, s], rc_s.at[k, s], rc_r.at[k, s], c_peer)

    def with_core(k, s):
        yy = y + s * (1 - 2 * y)
        mine = partial(index(zs[k], yy, c))
        arrived(crecv.at[k, s], rc_s.at[k, s], rc_r.at[k, s], c_peer)
        return mine + crecv[k, s].astype(F32)

    def with_y(k):
        mine = with_core(k, 0)
        arrived(yrecv.at[k], ry_s.at[k], ry_r.at[k], y_peer)
        return mine + yrecv[k].astype(F32)

    for k in order:
        to_core(k, 1)
    for k in order:
        ysend[k] = with_core(k, 1).astype(BF16)
        send(ysend.at[k], yrecv.at[k], ry_s.at[k], ry_r.at[k], y_peer)
    for k in order:
        to_core(k, 0)
    for k in order[:-1]:
        zsend[k] = with_y(k).astype(BF16)
        send(zsend.at[k], zrecv.at[k], rz_s.at[k], rz_r.at[k], z_peer[k])
    mine = with_y(0)
    for k in range(1, nz):
        arrived(zrecv.at[k], rz_s.at[k], rz_r.at[k], z_peer[k])
        mine = mine + zrecv[k].astype(F32)
    col_block(me)[...] = mine.astype(BF16)

    gather(col_block, (bz_s, bz_r, by_s, by_r, bc_s, bc_r), lambda k: None, lambda i: None)
    out_copy = pltpu.make_async_copy(proj_v, proj_hbm, out_sem)
    out_copy.start()
    for copy in sent:
        copy.wait_send()
    out_copy.wait()


def per_device(n, tokens, rotation_flip, gate_up, quant_codes, quant_exps, down_rows):
    own_rows, width = tokens.shape
    count = own_rows * n
    hidden, out_width = down_rows.shape
    group = width // quant_exps.shape[1]
    nz, cols = n // 4, out_width // n
    had = min(256, width)
    dma = pltpu.SemaphoreType.DMA
    vmem, hbm = pl.BlockSpec(memory_space=pltpu.VMEM), pl.BlockSpec(memory_space=pl.ANY)
    block = (count, cols)
    per_gather = [dma((nz,))] * 4 + [dma((nz, 2))] * 2
    hid_quant, projected = pl.pallas_call(
        functools.partial(kernel, n, group),
        out_shape=(
            jax.ShapeDtypeStruct((count, hidden), BF16),
            jax.ShapeDtypeStruct((count, out_width), BF16),
        ),
        in_specs=[vmem] * 4 + [hbm] * 3,
        out_specs=(vmem, hbm),
        scratch_shapes=[
            pltpu.VMEM(gate_up.shape, BF16),
            pltpu.VMEM(quant_codes.shape, BF16),
            pltpu.VMEM(down_rows.shape, BF16),
            pltpu.VMEM((count, width), BF16),
            pltpu.VMEM((count, width), BF16),
            pltpu.VMEM((count, hidden), BF16),
            pltpu.VMEM((count, out_width), BF16),
            pltpu.VMEM((nz, 2) + block, BF16),
            pltpu.VMEM((nz, 2) + block, BF16),
            pltpu.VMEM((nz,) + block, BF16),
            pltpu.VMEM((nz,) + block, BF16),
            pltpu.VMEM((nz,) + block, BF16),
            pltpu.VMEM((nz,) + block, BF16),
            dma((2, 4)),
            dma((2,)),
            dma,
            dma,
        ] + per_gather * 3,
        compiler_params=pltpu.CompilerParams(
            collective_id=0, has_side_effects=True, vmem_limit_bytes=62 * 2**20
        ),
        cost_estimate=pl.CostEstimate(
            flops=10 * count * width * hidden, bytes_accessed=50 * 2**20, transcendentals=0
        ),
    )(
        tokens, rotation_flip.reshape(1, width), jnp.asarray(hadamard_block(had), BF16),
        quant_exps, gate_up, quant_codes, down_rows,
    )
    gram = lax.dot_general(
        hid_quant, projected, (((0,), (0,)), ((), ())), preferred_element_type=F32
    )
    return (gram * (1.0 / count**0.5)).astype(BF16)


def solution(mesh):
    placed = (
        P(("dom", "tok"), None),
        P(),
        P("dom", None, "tok"),
        P("dom", None, "tok"),
        P("dom", None, "tok"),
        P(("dom", "tok"), None),
    )
    return jax.shard_map(
        functools.partial(per_device, mesh.shape["tok"]),
        mesh=mesh, in_specs=placed, out_specs=P(("dom", "tok"), None), check_vma=False,
    )
```

```python
import functools

import jax
import jax.numpy as jnp
import numpy as np
from jax import lax
from jax.experimental import pallas as pl
from jax.experimental.pallas import tpu as pltpu
from jax.sharding import PartitionSpec as P

MESH = pl.DeviceIdType.MESH
F32 = jnp.float32
BF16 = jnp.bfloat16


def hadamard_block(order):
    index = np.arange(order)
    common = index[:, None] & index[None, :]
    parity = np.zeros((order, order), np.int32)
    for bit_pos in range(order.bit_length()):
        parity ^= (common >> bit_pos) & 1
    return (1 - 2 * parity).astype(np.float32)


def xor(value, mask):
    out, bit = value, 1
    while bit <= mask:
        if mask & bit:
            out = out + bit * (1 - 2 * ((value // bit) % 2))
        bit *= 2
    return out


def kernel(
    n, group,
    tok_ref, flip_ref, had_ref, exps_ref, gu_hbm, codes_hbm, down_hbm,
    hidq_ref, proj_hbm,
    gu_v, codes_v, down_v, tok_v, rot_v, mis_v, proj_v,
    csend, crecv, ysend, yrecv, zsend, zrecv,
    codes_sem, gu_sem, down_sem, out_sem,
    az_s, az_r, ay_s, ay_r, ac_s, ac_r,
    bz_s, bz_r, by_s, by_r, bc_s, bc_r,
    rz_s, rz_r, ry_s, ry_r, rc_s, rc_r,
):
    nz = n // 4
    me = lax.axis_index("tok")
    z, y, c = me // 4, (me // 2) % 2, me % 2
    own_rows, width = tok_ref.shape
    tokens = own_rows * n
    hidden = mis_v.shape[1]
    cols = proj_v.shape[1] // n

    def index(zz, yy, cc):
        return (zz * 2 + yy) * 2 + cc

    zs = [xor(z, k) for k in range(nz)]
    z_peer = [index(zs[k], y, c) for k in range(nz)]
    y_peer, c_peer = index(z, 1 - y, c), index(z, y, 1 - c)

    chunks = codes_sem.shape[1]
    depth = width // chunks
    code_copies = [
        pltpu.make_async_copy(
            codes_hbm.at[p, pl.ds(q * depth, depth)],
            codes_v.at[p, pl.ds(q * depth, depth)],
            codes_sem.at[p, q],
        )
        for p in range(2) for q in range(chunks)
    ]
    gu_copies = [
        pltpu.make_async_copy(gu_hbm.at[p], gu_v.at[p], gu_sem.at[p]) for p in range(2)
    ]
    down_copy = pltpu.make_async_copy(down_hbm, down_v, down_sem)
    for copy in code_copies:
        copy.start()

    def row_block(i):
        return tok_v.at[pl.ds(pl.multiple_of(i * own_rows, own_rows), own_rows)]

    def col_block(i):
        return proj_v.at[:, pl.ds(pl.multiple_of(i * cols, cols), cols)]

    row_block(me)[...] = tok_ref[...]

    barrier = pltpu.get_barrier_semaphore()
    peers = z_peer[1:] + [y_peer, c_peer]
    for peer in peers:
        pl.semaphore_signal(barrier, inc=1, device_id={"tok": peer}, device_id_type=MESH)
    pl.semaphore_wait(barrier, len(peers))

    sent = []

    def send(src, dst, ssem, rsem, peer):
        copy = pltpu.make_async_remote_copy(
            src_ref=src, dst_ref=dst, send_sem=ssem, recv_sem=rsem,
            device_id={"tok": peer}, device_id_type=MESH,
        )
        copy.start()
        sent.append(copy)

    def arrived(dst, ssem, rsem, peer):
        pltpu.make_async_remote_copy(
            src_ref=dst, dst_ref=dst, send_sem=ssem, recv_sem=rsem,
            device_id={"tok": peer}, device_id_type=MESH,
        ).wait_recv()

    def gather(block, sems, between, landed):
        z_s, z_r, y_s, y_r, c_s, c_r = sems

        def on_y(k):
            i = index(zs[k], 1 - y, c)
            arrived(block(i), y_s.at[k], y_r.at[k], y_peer)
            send(block(i), block(i), c_s.at[k, 1], c_r.at[k, 1], c_peer)
            landed(i)

        def out(k):
            i = z_peer[k]
            send(block(i), block(i), y_s.at[k], y_r.at[k], y_peer)
            send(block(i), block(i), c_s.at[k, 0], c_r.at[k, 0], c_peer)
            landed(i)

        for k in range(nz - 1, 0, -1):
            send(block(me), block(me), z_s.at[k], z_r.at[k], z_peer[k])
        out(0)
        between(0)
        for k in range(1, nz):
            arrived(block(z_peer[k]), z_s.at[k], z_r.at[k], z_peer[k])
            out(k)
            on_y(k - 1)
            between(k)
        on_y(nz - 1)
        for k in range(nz):
            for s in range(2):
                i = index(zs[k], y + s * (1 - 2 * y), 1 - c)
                arrived(block(i), c_s.at[k, s], c_r.at[k, s], c_peer)
                landed(i)

    def scale_chunk(t):
        p, q = t // chunks, t % chunks
        code_copies[t].wait()

        def one(step, carry):
            g = q * (depth // group) + step
            scale = jnp.exp2(exps_ref[p, pl.ds(g, 1), :].astype(F32))
            tile = jnp.broadcast_to(scale, (16, hidden)).astype(BF16)
            for r in range(group // 16):
                rows = pl.ds(pl.multiple_of(g * group + r * 16, 16), 16)
                codes_v[p, rows, :] = codes_v[p, rows, :] * tile
            return carry

        lax.fori_loop(0, depth // group, one, 0)

    total = 2 * chunks
    marks = [total // 2 + (total - total // 2) * k // (nz - 1) for k in range(nz)]

    def between(k):
        for t in range(marks[k - 1] if k else 0, marks[k]):
            scale_chunk(t)
        if k == 0:
            for copy in gu_copies + [down_copy]:
                copy.start()

    gather(row_block, (az_s, az_r, ay_s, ay_r, ac_s, ac_r), between, lambda i: None)

    had = had_ref.shape[0]
    sign = (1 - 2 * flip_ref[...]).astype(F32).astype(BF16)
    table = had_ref[...]
    span = min(64, tokens)

    def rotate(step, carry):
        rows = pl.ds(pl.multiple_of(step * span, span), span)
        parts = []
        for b in range(width // had):
            lanes = slice(b * had, (b + 1) * had)
            signed = tok_v[rows, lanes] * sign[:, lanes]
            parts.append(jnp.dot(signed, table, preferred_element_type=F32))
        half = 1
        while half < len(parts):
            for b in range(len(parts)):
                if not b & half:
                    low, high = parts[b], parts[b + half]
                    parts[b], parts[b + half] = low + high, low - high
            half *= 2
        for b in range(width // had):
            rot_v[rows, b * had:(b + 1) * had] = (parts[b] * (1.0 / width**0.5)).astype(BF16)
        return carry

    lax.fori_loop(0, tokens // span, rotate, 0)

    for copy in gu_copies:
        copy.wait()
    tile = 256

    def swiglu(lhs, w, lanes):
        gate = jnp.dot(lhs[...], w[0, :, lanes], preferred_element_type=F32)
        upper = jnp.dot(lhs[...], w[1, :, lanes], preferred_element_type=F32)
        return (gate / (1.0 + jnp.exp(-gate)) * upper).astype(BF16)

    def hidden_tile(step, carry):
        lanes = pl.ds(pl.multiple_of(step * tile, tile), tile)
        full = swiglu(tok_v, gu_v, lanes)
        quant = swiglu(rot_v, codes_v, lanes)
        hidq_ref[:, lanes] = quant
        mis_v[:, lanes] = (full.astype(F32) - quant.astype(F32)).astype(BF16)
        return carry

    lax.fori_loop(0, hidden // tile, hidden_tile, 0)

    down_copy.wait()

    def partial(i):
        lanes = pl.ds(pl.multiple_of(i * cols, cols), cols)
        return jnp.dot(mis_v[...], down_v[:, lanes], preferred_element_type=F32)

    order = list(range(nz - 1, -1, -1))

    def to_core(k, s):
        yy = y + s * (1 - 2 * y)
        csend[k, s] = partial(index(zs[k], yy, 1 - c)).astype(BF16)
        send(csend.at[k, s], crecv.at[k, s], rc_s.at[k, s], rc_r.at[k, s], c_peer)

    def with_core(k, s):
        yy = y + s * (1 - 2 * y)
        mine = partial(index(zs[k], yy, c))
        arrived(crecv.at[k, s], rc_s.at[k, s], rc_r.at[k, s], c_peer)
        return mine + crecv[k, s].astype(F32)

    def with_y(k):
        mine = with_core(k, 0)
        arrived(yrecv.at[k], ry_s.at[k], ry_r.at[k], y_peer)
        return mine + yrecv[k].astype(F32)

    for k in order:
        to_core(k, 1)
    for k in order:
        ysend[k] = with_core(k, 1).astype(BF16)
        send(ysend.at[k], yrecv.at[k], ry_s.at[k], ry_r.at[k], y_peer)
    for k in order:
        to_core(k, 0)
    for k in order[:-1]:
        zsend[k] = with_y(k).astype(BF16)
        send(zsend.at[k], zrecv.at[k], rz_s.at[k], rz_r.at[k], z_peer[k])
    mine = with_y(0)
    for k in range(1, nz):
        arrived(zrecv.at[k], rz_s.at[k], rz_r.at[k], z_peer[k])
        mine = mine + zrecv[k].astype(F32)
    col_block(me)[...] = mine.astype(BF16)

    gather(col_block, (bz_s, bz_r, by_s, by_r, bc_s, bc_r), lambda k: None, lambda i: None)
    out_copy = pltpu.make_async_copy(proj_v, proj_hbm, out_sem)
    out_copy.start()
    for copy in sent:
        copy.wait_send()
    out_copy.wait()


def gram_kernel(factor, hid_ref, proj_ref, out_ref, turned):
    @pl.when(pl.program_id(0) == 0)
    def _():
        turned[...] = hid_ref[...].T

    gram = jnp.dot(turned[...], proj_ref[...], preferred_element_type=F32)
    out_ref[...] = (gram * factor).astype(BF16)


def per_device(n, tokens, rotation_flip, gate_up, quant_codes, quant_exps, down_rows):
    own_rows, width = tokens.shape
    count = own_rows * n
    hidden, out_width = down_rows.shape
    group = width // quant_exps.shape[1]
    nz, cols = n // 4, out_width // n
    had = min(256, width)
    dma = pltpu.SemaphoreType.DMA
    vmem, hbm = pl.BlockSpec(memory_space=pltpu.VMEM), pl.BlockSpec(memory_space=pl.ANY)
    block = (count, cols)
    per_gather = [dma((nz,))] * 4 + [dma((nz, 2))] * 2
    hid_quant, projected = pl.pallas_call(
        functools.partial(kernel, n, group),
        out_shape=(
            jax.ShapeDtypeStruct((count, hidden), BF16),
            jax.ShapeDtypeStruct((count, out_width), BF16),
        ),
        in_specs=[vmem] * 4 + [hbm] * 3,
        out_specs=(vmem, hbm),
        scratch_shapes=[
            pltpu.VMEM(gate_up.shape, BF16),
            pltpu.VMEM(quant_codes.shape, BF16),
            pltpu.VMEM(down_rows.shape, BF16),
            pltpu.VMEM((count, width), BF16),
            pltpu.VMEM((count, width), BF16),
            pltpu.VMEM((count, hidden), BF16),
            pltpu.VMEM((count, out_width), BF16),
            pltpu.VMEM((nz, 2) + block, BF16),
            pltpu.VMEM((nz, 2) + block, BF16),
            pltpu.VMEM((nz,) + block, BF16),
            pltpu.VMEM((nz,) + block, BF16),
            pltpu.VMEM((nz,) + block, BF16),
            pltpu.VMEM((nz,) + block, BF16),
            dma((2, 4)),
            dma((2,)),
            dma,
            dma,
        ] + per_gather * 3,
        compiler_params=pltpu.CompilerParams(
            collective_id=0, has_side_effects=True, vmem_limit_bytes=62 * 2**20
        ),
        cost_estimate=pl.CostEstimate(
            flops=10 * count * width * hidden, bytes_accessed=50 * 2**20, transcendentals=0
        ),
    )(
        tokens, rotation_flip.reshape(1, width), jnp.asarray(hadamard_block(had), BF16),
        quant_exps, gate_up, quant_codes, down_rows,
    )
    lanes = min(512, out_width)
    return pl.pallas_call(
        functools.partial(gram_kernel, 1.0 / count**0.5),
        out_shape=jax.ShapeDtypeStruct((hidden, out_width), BF16),
        grid=(out_width // lanes,),
        in_specs=[
            pl.BlockSpec((count, hidden), lambda i: (0, 0)),
            pl.BlockSpec((count, lanes), lambda i: (0, i)),
        ],
        out_specs=pl.BlockSpec((hidden, lanes), lambda i: (0, i)),
        scratch_shapes=[pltpu.VMEM((hidden, count), BF16)],
        compiler_params=pltpu.CompilerParams(vmem_limit_bytes=62 * 2**20),
    )(hid_quant, projected)


def solution(mesh):
    placed = (
        P(("dom", "tok"), None),
        P(),
        P("dom", None, "tok"),
        P("dom", None, "tok"),
        P("dom", None, "tok"),
        P(("dom", "tok"), None),
    )
    return jax.shard_map(
        functools.partial(per_device, mesh.shape["tok"]),
        mesh=mesh, in_specs=placed, out_specs=P(("dom", "tok"), None), check_vma=False,
    )
```

```python
import functools

import jax
import jax.numpy as jnp
import numpy as np
from jax import lax
from jax.experimental import pallas as pl
from jax.experimental.pallas import tpu as pltpu
from jax.sharding import PartitionSpec as P

MESH = pl.DeviceIdType.MESH
F32 = jnp.float32
BF16 = jnp.bfloat16


def hadamard_block(order):
    index = np.arange(order)
    common = index[:, None] & index[None, :]
    parity = np.zeros((order, order), np.int32)
    for bit_pos in range(order.bit_length()):
        parity ^= (common >> bit_pos) & 1
    return (1 - 2 * parity).astype(np.float32)


def xor(value, mask):
    out, bit = value, 1
    while bit <= mask:
        if mask & bit:
            out = out + bit * (1 - 2 * ((value // bit) % 2))
        bit *= 2
    return out


def kernel(
    n, group,
    tok_ref, flip_ref, had_ref, exps_ref, gu_hbm, codes_hbm, down_hbm,
    hidq_ref, proj_hbm,
    gu_v, codes_v, down_v, tok_v, rot_v, mis_v, proj_v,
    csend, crecv, ysend, yrecv, zsend, zrecv,
    codes_sem, gu_sem, down_sem, out_sem,
    az_s, az_r, ay_s, ay_r, ac_s, ac_r,
    bz_s, bz_r, by_s, by_r, bc_s, bc_r,
    rz_s, rz_r, ry_s, ry_r, rc_s, rc_r,
):
    nz = n // 4
    me = lax.axis_index("tok")
    z, y, c = me // 4, (me // 2) % 2, me % 2
    own_rows, width = tok_ref.shape
    tokens = own_rows * n
    hidden = mis_v.shape[1]
    cols = proj_v.shape[1] // n

    def index(zz, yy, cc):
        return (zz * 2 + yy) * 2 + cc

    zs = [xor(z, k) for k in range(nz)]
    z_peer = [index(zs[k], y, c) for k in range(nz)]
    y_peer, c_peer = index(z, 1 - y, c), index(z, y, 1 - c)

    chunks = codes_sem.shape[1]
    depth = width // chunks
    code_copies = [
        pltpu.make_async_copy(
            codes_hbm.at[p, pl.ds(q * depth, depth)],
            codes_v.at[p, pl.ds(q * depth, depth)],
            codes_sem.at[p, q],
        )
        for p in range(2) for q in range(chunks)
    ]
    gu_copies = [
        pltpu.make_async_copy(gu_hbm.at[p], gu_v.at[p], gu_sem.at[p]) for p in range(2)
    ]
    down_copy = pltpu.make_async_copy(down_hbm, down_v, down_sem)
    for copy in code_copies:
        copy.start()

    def row_block(i):
        return tok_v.at[pl.ds(pl.multiple_of(i * own_rows, own_rows), own_rows)]

    def col_block(i):
        return proj_v.at[:, pl.ds(pl.multiple_of(i * cols, cols), cols)]

    row_block(me)[...] = tok_ref[...]

    barrier = pltpu.get_barrier_semaphore()
    peers = z_peer[1:] + [y_peer, c_peer]
    for peer in peers:
        pl.semaphore_signal(barrier, inc=1, device_id={"tok": peer}, device_id_type=MESH)
    pl.semaphore_wait(barrier, len(peers))

    sent = []

    def send(src, dst, ssem, rsem, peer):
        copy = pltpu.make_async_remote_copy(
            src_ref=src, dst_ref=dst, send_sem=ssem, recv_sem=rsem,
            device_id={"tok": peer}, device_id_type=MESH,
        )
        copy.start()
        sent.append(copy)

    def arrived(dst, ssem, rsem, peer):
        pltpu.make_async_remote_copy(
            src_ref=dst, dst_ref=dst, send_sem=ssem, recv_sem=rsem,
            device_id={"tok": peer}, device_id_type=MESH,
        ).wait_recv()

    def gather(block, sems, between, landed):
        z_s, z_r, y_s, y_r, c_s, c_r = sems

        def on_y(k):
            i = index(zs[k], 1 - y, c)
            arrived(block(i), y_s.at[k], y_r.at[k], y_peer)
            send(block(i), block(i), c_s.at[k, 1], c_r.at[k, 1], c_peer)
            landed(i)

        def out(k):
            i = z_peer[k]
            send(block(i), block(i), y_s.at[k], y_r.at[k], y_peer)
            send(block(i), block(i), c_s.at[k, 0], c_r.at[k, 0], c_peer)
            landed(i)

        for k in range(1, nz):
            send(block(me), block(me), z_s.at[k], z_r.at[k], z_peer[k])
        out(0)
        between(0)
        for k in range(1, nz):
            arrived(block(z_peer[k]), z_s.at[k], z_r.at[k], z_peer[k])
            out(k)
            on_y(k - 1)
            between(k)
        on_y(nz - 1)
        for k in range(nz):
            for s in range(2):
                i = index(zs[k], y + s * (1 - 2 * y), 1 - c)
                arrived(block(i), c_s.at[k, s], c_r.at[k, s], c_peer)
                landed(i)

    def scale_chunk(t):
        p, q = t // chunks, t % chunks
        code_copies[t].wait()

        def one(step, carry):
            g = q * (depth // group) + step
            scale = jnp.exp2(exps_ref[p, pl.ds(g, 1), :].astype(F32))
            tile = jnp.broadcast_to(scale, (16, hidden)).astype(BF16)
            for r in range(group // 16):
                rows = pl.ds(pl.multiple_of(g * group + r * 16, 16), 16)
                codes_v[p, rows, :] = codes_v[p, rows, :] * tile
            return carry

        lax.fori_loop(0, depth // group, one, 0)

    total = 2 * chunks
    marks = [total // 2 + (total - total // 2) * k // (nz - 1) for k in range(nz)]

    def between(k):
        for t in range(marks[k - 1] if k else 0, marks[k]):
            scale_chunk(t)
        if k == 0:
            for copy in gu_copies + [down_copy]:
                copy.start()

    gather(row_block, (az_s, az_r, ay_s, ay_r, ac_s, ac_r), between, lambda i: None)

    had = had_ref.shape[0]
    sign = (1 - 2 * flip_ref[...]).astype(F32).astype(BF16)
    table = had_ref[...]
    span = min(64, tokens)

    def rotate(step, carry):
        rows = pl.ds(pl.multiple_of(step * span, span), span)
        parts = []
        for b in range(width // had):
            lanes = slice(b * had, (b + 1) * had)
            signed = tok_v[rows, lanes] * sign[:, lanes]
            parts.append(jnp.dot(signed, table, preferred_element_type=F32))
        half = 1
        while half < len(parts):
            for b in range(len(parts)):
                if not b & half:
                    low, high = parts[b], parts[b + half]
                    parts[b], parts[b + half] = low + high, low - high
            half *= 2
        for b in range(width // had):
            rot_v[rows, b * had:(b + 1) * had] = (parts[b] * (1.0 / width**0.5)).astype(BF16)
        return carry

    lax.fori_loop(0, tokens // span, rotate, 0)

    for copy in gu_copies:
        copy.wait()
    tile = 256

    def swiglu(lhs, w, lanes):
        gate = jnp.dot(lhs[...], w[0, :, lanes], preferred_element_type=F32)
        upper = jnp.dot(lhs[...], w[1, :, lanes], preferred_element_type=F32)
        return (gate / (1.0 + jnp.exp(-gate)) * upper).astype(BF16)

    def hidden_tile(step, carry):
        lanes = pl.ds(pl.multiple_of(step * tile, tile), tile)
        full = swiglu(tok_v, gu_v, lanes)
        quant = swiglu(rot_v, codes_v, lanes)
        hidq_ref[:, lanes] = quant
        mis_v[:, lanes] = (full.astype(F32) - quant.astype(F32)).astype(BF16)
        return carry

    lax.fori_loop(0, hidden // tile, hidden_tile, 0)

    down_copy.wait()

    def partial(i):
        lanes = pl.ds(pl.multiple_of(i * cols, cols), cols)
        return jnp.dot(mis_v[...], down_v[:, lanes], preferred_element_type=F32)

    order = list(range(nz - 1, -1, -1))

    def to_core(k, s):
        yy = y + s * (1 - 2 * y)
        csend[k, s] = partial(index(zs[k], yy, 1 - c)).astype(BF16)
        send(csend.at[k, s], crecv.at[k, s], rc_s.at[k, s], rc_r.at[k, s], c_peer)

    def with_core(k, s):
        yy = y + s * (1 - 2 * y)
        mine = partial(index(zs[k], yy, c))
        arrived(crecv.at[k, s], rc_s.at[k, s], rc_r.at[k, s], c_peer)
        return mine + crecv[k, s].astype(F32)

    def with_y(k):
        mine = with_core(k, 0)
        arrived(yrecv.at[k], ry_s.at[k], ry_r.at[k], y_peer)
        return mine + yrecv[k].astype(F32)

    for k in order:
        to_core(k, 1)
    for k in order:
        ysend[k] = with_core(k, 1).astype(BF16)
        send(ysend.at[k], yrecv.at[k], ry_s.at[k], ry_r.at[k], y_peer)
    for k in order:
        to_core(k, 0)
    for k in order[:-1]:
        zsend[k] = with_y(k).astype(BF16)
        send(zsend.at[k], zrecv.at[k], rz_s.at[k], rz_r.at[k], z_peer[k])
    mine = with_y(0)
    for k in range(1, nz):
        arrived(zrecv.at[k], rz_s.at[k], rz_r.at[k], z_peer[k])
        mine = mine + zrecv[k].astype(F32)
    col_block(me)[...] = mine.astype(BF16)

    gather(col_block, (bz_s, bz_r, by_s, by_r, bc_s, bc_r), lambda k: None, lambda i: None)
    out_copy = pltpu.make_async_copy(proj_v, proj_hbm, out_sem)
    out_copy.start()
    for copy in sent:
        copy.wait_send()
    out_copy.wait()


def per_device(n, tokens, rotation_flip, gate_up, quant_codes, quant_exps, down_rows):
    own_rows, width = tokens.shape
    count = own_rows * n
    hidden, out_width = down_rows.shape
    group = width // quant_exps.shape[1]
    nz, cols = n // 4, out_width // n
    had = min(256, width)
    dma = pltpu.SemaphoreType.DMA
    vmem, hbm = pl.BlockSpec(memory_space=pltpu.VMEM), pl.BlockSpec(memory_space=pl.ANY)
    block = (count, cols)
    per_gather = [dma((nz,))] * 4 + [dma((nz, 2))] * 2
    hid_quant, projected = pl.pallas_call(
        functools.partial(kernel, n, group),
        out_shape=(
            jax.ShapeDtypeStruct((count, hidden), BF16),
            jax.ShapeDtypeStruct((count, out_width), BF16),
        ),
        in_specs=[vmem] * 4 + [hbm] * 3,
        out_specs=(vmem, hbm),
        scratch_shapes=[
            pltpu.VMEM(gate_up.shape, BF16),
            pltpu.VMEM(quant_codes.shape, BF16),
            pltpu.VMEM(down_rows.shape, BF16),
            pltpu.VMEM((count, width), BF16),
            pltpu.VMEM((count, width), BF16),
            pltpu.VMEM((count, hidden), BF16),
            pltpu.VMEM((count, out_width), BF16),
            pltpu.VMEM((nz, 2) + block, BF16),
            pltpu.VMEM((nz, 2) + block, BF16),
            pltpu.VMEM((nz,) + block, BF16),
            pltpu.VMEM((nz,) + block, BF16),
            pltpu.VMEM((nz,) + block, BF16),
            pltpu.VMEM((nz,) + block, BF16),
            dma((2, 4)),
            dma((2,)),
            dma,
            dma,
        ] + per_gather * 3,
        compiler_params=pltpu.CompilerParams(
            collective_id=0, has_side_effects=True, vmem_limit_bytes=62 * 2**20
        ),
        cost_estimate=pl.CostEstimate(
            flops=10 * count * width * hidden, bytes_accessed=50 * 2**20, transcendentals=0
        ),
    )(
        tokens, rotation_flip.reshape(1, width), jnp.asarray(hadamard_block(had), BF16),
        quant_exps, gate_up, quant_codes, down_rows,
    )
    gram = lax.dot_general(
        hid_quant, projected, (((0,), (0,)), ((), ())), preferred_element_type=F32
    )
    return (gram * (1.0 / count**0.5)).astype(BF16)


def solution(mesh):
    placed = (
        P(("dom", "tok"), None),
        P(),
        P("dom", None, "tok"),
        P("dom", None, "tok"),
        P("dom", None, "tok"),
        P(("dom", "tok"), None),
    )
    return jax.shard_map(
        functools.partial(per_device, mesh.shape["tok"]),
        mesh=mesh, in_specs=placed, out_specs=P(("dom", "tok"), None), check_vma=False,
    )
```
